32 devices in a mesh: space: 8 (over y, x, core), mode: 4 (over z).
Axes of the slice: x: 2, y: 2, z: 4, core: 2. Of those that a mesh axis runs over, the one named last changes fastest.
Arguments:
- mode_fields: float32 [3, 128, 8, 512], P(None, 'mode', 'space'), may hold values from -2.5 to 2.5
- volume: float32 [8, 512], P('space'), may hold values from 0.25 to 4
- fluid_mask: int32 [8, 512], P('space'), may hold values 0 or 1
Outputs:
- convection: float32 [128, 128, 128], P('space', None, 'mode')
The draws below stay inside these ranges and needn't reach their ends.
All inputs are finite; a program needn't handle non-finite values. No bound on the sum of `fluid_mask` on one device may be relied on, other than what follows from the above.
Results may differ from the reference program's by a relative error of at most 0.0001.
Values sent between devices are 32-bit elements; how exact they have to be, the bound alone decides.
No kernel may reach another device: no remote copies, remote signals or barrier semaphores. Data moves between devices by JAX's collectives and lax.ppermute only.
A program may use at most 128 MiB of HBM per device.

```python
import math
import jax
import jax.numpy as jnp
from jax import lax

M = 128
TGY = 8
TX = 4
TY = 16
TZ = 8
TGX = 1
CELLS = 512
NX = 4
NY = 128
NZ = 8
N_SPACE = 8


def touch_ends(entries, stream_key, low, largest):
    longest = entries.shape.index(max(entries.shape))
    spots = []
    for shift in (0, 1):
        where = [jax.random.randint(jax.random.fold_in(stream_key, axis), (), 0, length) for axis, length in enumerate(entries.shape)]
        where[longest] = (where[longest] + shift) % entries.shape[longest]
        spots.append(tuple(where))
    return entries.at[spots[0]].set(low).at[spots[1]].set(largest)


def steps_of(rng, shape, cuts, smallest, largest):
    level = 1.0
    for dim, shards_of in cuts:
        heights = jax.random.uniform(jax.random.fold_in(jax.random.fold_in(rng, 6), dim), (shards_of,), jnp.float32, smallest / len(cuts), largest / len(cuts))
        level = level * jnp.repeat(jnp.exp(heights), shape[dim] // shards_of).reshape((-1,) + (1,) * (len(shape) - 1 - dim))
    return level


def noise(stream_key, shape, deviation, limit, pieces=(), held_as=jnp.bfloat16):
    result = jax.random.normal(stream_key, shape, jnp.float32) * deviation
    if len(pieces) > 0:
        result = steps_of(stream_key, shape, pieces, -0.22, 0.18) * result
    return jnp.clip(result, min=-limit, max=limit).astype(held_as)


def setup_inputs(seed: int = 0) -> dict:
    splits = jax.random.split(jax.random.key(seed), 4)
    return {
        "mode_fields": noise(splits[0], (3, M, N_SPACE, CELLS), ((9 * NX * NY * NZ) ** -0.1667), 2.5, ((1, 4), (2, 8)), jnp.float32),
        "volume": jnp.clip(jnp.exp(math.log(4.0) - 2.7725887 * jax.random.uniform(splits[1], (N_SPACE, CELLS), jnp.float32) ** steps_of(splits[1], (N_SPACE, CELLS), ((0, 8),), -0.2, 0.2)), 0.25, 4.0),
        "fluid_mask": touch_ends((jax.random.randint(splits[2], (N_SPACE, CELLS), 0, 8) < 7).astype(jnp.int32), jax.random.fold_in(splits[2], 1), 0, 1),
    }


def derivative(padded, axis, length):
    def shifted(offset):
        return lax.slice_in_dim(padded, 2 + offset, 2 + offset + length, axis=axis)
    return (8.0 * (shifted(1) - shifted(-1)) - (shifted(2) - shifted(-2))) / 12.0


def reference(mode_fields, volume, fluid_mask):
    grid = mode_fields.reshape(3, M, TGX, TGY, TX, TY, TZ)
    grid = grid.transpose(0, 1, 2, 4, 3, 5, 6).reshape(3, M, NX, NY, NZ)
    padded = jnp.pad(grid, ((0, 0), (0, 0), (2, 2), (2, 2), (2, 2)))
    along_x = derivative(padded[:, :, :, 2:-2, 2:-2], 2, NX)
    along_y = derivative(padded[:, :, 2:-2, :, 2:-2], 3, NY)
    along_z = derivative(padded[:, :, 2:-2, 2:-2, :], 4, NZ)
    gradient = jnp.stack([along_x, along_y, along_z])
    gradient = gradient.reshape(3, 3, M, TGX, TX, TGY, TY, TZ)
    gradient = gradient.transpose(0, 1, 2, 3, 5, 4, 6, 7).reshape(3, 3, M, N_SPACE, CELLS)
    weights = volume * fluid_mask.astype(jnp.float32)
    tile_fields = jnp.moveaxis(mode_fields, 2, 0)
    tile_gradient = jnp.moveaxis(gradient, 3, 0)

    def accumulate(total, slices):
        fields, grads, tile_weights = slices
        advected = jnp.einsum('ejc,edkc->djkc', fields, grads, precision=lax.Precision.HIGHEST)
        term = jnp.einsum('dic,djkc->ijk', fields * tile_weights, advected, precision=lax.Precision.HIGHEST)
        return total + term, None

    start_total = jnp.zeros((M, M, M), jnp.float32)
    convection, unused = lax.scan(accumulate, start_total, (tile_fields, tile_gradient, weights))
    return convection
```

```python
import functools

import jax
import jax.numpy as jnp
from jax import lax
from jax.experimental import pallas as pl
from jax.experimental.pallas import tpu as pltpu
from jax.sharding import PartitionSpec as P

M = 128
TGY = 8
TX = 4
TY = 16
TZ = 8


def passed_along(value, axis, by):
    devices = lax.axis_size(axis)
    pairs = [(i, i + by) for i in range(devices) if 0 <= i + by < devices]
    return lax.ppermute(value, axis, pairs)


def derivative(padded, axis, length):

    def shifted(offset):
        return lax.slice_in_dim(padded, 2 + offset, 2 + offset + length, axis=axis)

    return (8.0 * (shifted(1) - shifted(-1)) - (shifted(2) - shifted(-2))) / 12.0


def neighbour(rim_block, offset):
    return passed_along(rim_block, "space", offset)


def per_device_general(mode_fields, volume, fluid_mask):
    k_count = mode_fields.shape[1]
    cell_count = mode_fields.shape[3]
    rim_rows = 3 * k_count
    own_block = mode_fields.reshape(3, k_count, TX, TY, TZ)
    upper_x = own_block[:, :, TX - 2 :].reshape(rim_rows, 2 * TY * TZ)
    lower_x = own_block[:, :, :2].reshape(rim_rows, 2 * TY * TZ)
    upper_y = own_block[:, :, :, TY - 2 :].reshape(rim_rows, TX * 2 * TZ)
    lower_y = own_block[:, :, :, :2].reshape(rim_rows, TX * 2 * TZ)
    below_x = neighbour(upper_x, TGY).reshape(3, k_count, 2, TY, TZ)
    above_x = neighbour(lower_x, -TGY).reshape(3, k_count, 2, TY, TZ)
    tile_column = lax.axis_index("space") % TGY
    below_y = neighbour(upper_y, 1).reshape(3, k_count, TX, 2, TZ)
    above_y = neighbour(lower_y, -1).reshape(3, k_count, TX, 2, TZ)
    below_y = jnp.where(tile_column > 0, below_y, jnp.zeros_like(below_y))
    above_y = jnp.where(tile_column < TGY - 1, above_y, jnp.zeros_like(above_y))
    padded_x = jnp.concatenate([below_x, own_block, above_x], axis=2)
    padded_y = jnp.concatenate([below_y, own_block, above_y], axis=3)
    padded_z = jnp.pad(own_block, ((0, 0), (0, 0), (0, 0), (0, 0), (2, 2)))
    gradient = jnp.stack(
        [derivative(padded_x, 2, TX), derivative(padded_y, 3, TY), derivative(padded_z, 4, TZ)]
    )
    gradient = gradient.reshape(3, 3, k_count, cell_count)
    weights = (volume * fluid_mask.astype(jnp.float32)).reshape(cell_count)
    own_fields = mode_fields.reshape(3, k_count, cell_count)
    everything = lax.all_gather(own_fields, "mode", axis=1, tiled=True)
    weighted = everything * weights
    block_width = min(64, M)
    pieces = []
    for block_start in range(0, M, block_width):
        advected = jnp.einsum(
            "ejc,edkc->djkc",
            everything[:, block_start : block_start + block_width],
            gradient,
            precision=lax.Precision.HIGHEST,
        )
        pieces.append(
            jnp.einsum("dic,djkc->ijk", weighted, advected, precision=lax.Precision.HIGHEST)
        )
    partial_tensor = jnp.concatenate(pieces, axis=1)
    return lax.psum_scatter(partial_tensor, "space", scatter_dimension=0, tiled=True)


LANES = TY * TZ
CELLS = TX * LANES
F32 = jnp.float32
BF16 = jnp.bfloat16
MIB = 1 << 20


def on_chip(kernel, out_shape, scratch=(), flops=0, limit=48):
    outs = out_shape if isinstance(out_shape, (list, tuple)) else [out_shape]

    def call(*operands):
        moved = sum(a.size * a.dtype.itemsize for a in list(operands) + list(outs))
        return pl.pallas_call(
            kernel,
            out_shape=out_shape,
            in_specs=[pl.BlockSpec(memory_space=pltpu.VMEM)] * len(operands),
            out_specs=jax.tree.map(lambda _: pl.BlockSpec(memory_space=pltpu.VMEM), out_shape),
            scratch_shapes=list(scratch),
            compiler_params=pltpu.CompilerParams(vmem_limit_bytes=limit * MIB),
            cost_estimate=pl.CostEstimate(flops=flops, bytes_accessed=moved, transcendentals=0),
        )(*operands)

    return call


def lane_index(rows):
    return lax.broadcasted_iota(jnp.int32, (rows, LANES), 1)


def rim_kernel(own_ref, rim_ref):
    rows = rim_ref.shape[0]
    upper = lax.axis_index("space") % 2 == 1
    lane = lane_index(rows)
    width = 2 * TZ
    total = jnp.zeros((rows, LANES), F32)
    for x in range(TX):
        chunk = own_ref[pl.ds(x, rows, stride=TX), :]
        first = pltpu.roll(chunk, (width * x) % LANES, 1)
        last = pltpu.roll(chunk, (width * x + width) % LANES, 1)
        inside = (lane >= width * x) & (lane < width * (x + 1))
        total = jnp.where(inside, jnp.where(upper, last, first), total)
    rim_ref[...] = total


def gradient_kernel(own_ref, beside_ref, rim_ref, rim_beside_ref, grad_ref):
    k_count = grad_ref.shape[3]
    odd = lax.axis_index("space") % 2
    upper = odd == 1
    lane = lane_index(k_count)
    in_z = lane % TZ
    width = 2 * TZ

    def back(value, by):
        return pltpu.roll(value, by, 1)

    def ahead(value, by):
        return pltpu.roll(value, LANES - by, 1)

    def central(plus1, minus1, plus2, minus2):
        return (8.0 * (plus1 - minus1) - (plus2 - minus2)) / 12.0

    zero = jnp.zeros((k_count, LANES), F32)
    for d in range(3):
        start = d * k_count * TX
        own = [own_ref[pl.ds(start + x, k_count, stride=TX), :] for x in range(TX)]
        beside = [beside_ref[pl.ds(start + x, k_count, stride=TX), :] for x in range(TX)]
        rim = rim_ref[pl.ds(d * k_count, k_count), :]
        rim_beside = rim_beside_ref[pl.ds(d * k_count, k_count), :]
        low = [jnp.where(upper, b, a) for a, b in zip(own, beside)]
        high = [jnp.where(upper, a, b) for a, b in zip(own, beside)]
        rim_low = jnp.where(upper, rim_beside, rim)
        rim_high = jnp.where(upper, rim, rim_beside)
        for tile, here in ((odd, low), (1 - odd, high)):
            for x in range(TX):
                cells = pl.ds(x * LANES, LANES)
                now = here[x]
                if here is low:
                    before = pltpu.roll(rim_low, (LANES - width - width * x) % LANES, 1)
                    after = high[x]
                else:
                    before = low[x]
                    after = pltpu.roll(rim_high, (LANES - width * x) % LANES, 1)
                at = [here[x + o] if 0 <= x + o < TX else zero for o in (1, -1, 2, -2)]
                grad_ref[tile, 0, d, :, cells] = central(*at)
                grad_ref[tile, 1, d, :, cells] = central(
                    jnp.where(lane >= LANES - TZ, ahead(after, TZ), ahead(now, TZ)),
                    jnp.where(lane < TZ, back(before, TZ), back(now, TZ)),
                    jnp.where(lane >= LANES - width, ahead(after, width), ahead(now, width)),
                    jnp.where(lane < width, back(before, width), back(now, width)),
                )
                grad_ref[tile, 2, d, :, cells] = central(
                    jnp.where(in_z < TZ - 1, ahead(now, 1), 0.0),
                    jnp.where(in_z >= 1, back(now, 1), 0.0),
                    jnp.where(in_z < TZ - 2, ahead(now, 2), 0.0),
                    jnp.where(in_z >= 2, back(now, 2), 0.0),
                )


def split(value):
    high = value.astype(BF16)
    return high, (value - high.astype(F32)).astype(BF16)


def assemble_kernel(steps, *refs):
    own, beside, weights, weights_beside = refs[:4]
    first, second = refs[4 : 4 + steps], refs[4 + steps : 4 + 2 * steps]
    first_swapped, second_swapped = refs[4 + 2 * steps : 4 + 3 * steps], refs[4 + 3 * steps : 4 + 4 * steps]
    right_ref, left_ref, fields = refs[4 + 4 * steps :]
    odd = lax.axis_index("space") % 2
    place = lax.axis_index("mode")
    block = own.shape[0] // 3
    k_count = block // TX
    blocks = steps + 1
    modes = k_count * blocks

    def put(tile, index, source):
        for d in range(3):
            begin = pl.multiple_of(d * modes * TX + index * block, block)
            fields[tile, pl.ds(begin, block), :] = source[pl.ds(d * block, block), :]

    put(0, place, own)
    put(1, place, beside)
    for hop in range(1, blocks):
        below, above = place - hop, place + hop
        for tile, direct, swapped in ((0, first, second_swapped), (1, second, first_swapped)):
            for from_core, source in ((0, direct), (1, swapped)):
                @pl.when((odd == from_core) & (below >= 0))
                def _(tile=tile, source=source, below=below, hop=hop):
                    put(tile, below, source[hop - 1])

                @pl.when((odd != from_core) & (above < blocks))
                def _(tile=tile, source=source, above=above, hop=hop):
                    put(tile, above, source[hop - 1])

    chips, shares = left_ref.shape[2:4]
    for tile, weight in ((0, weights), (1, weights_beside)):
        for d in range(3):
            for x in range(TX):
                cells = pl.ds(x * LANES, LANES)
                chunk = fields[tile, pl.ds(d * modes * TX + x, modes, stride=TX), :]
                high, low = split(chunk.T)
                right_ref[tile, d, cells, pl.ds(0, modes)] = high
                right_ref[tile, d, cells, pl.ds(modes, modes)] = low
                for q in range(chips):
                    begin = (d * modes + (2 * q + odd) * shares) * TX + x
                    rows = fields[tile, pl.ds(begin, shares, stride=TX), :]
                    left_ref[tile, d, q, :, cells] = rows * weight[pl.ds(x, 1), :]


def tensor_kernel(apart, left_ref, grad_ref, right_ref, out_ref, total):
    k_count = grad_ref.shape[3]
    shares = out_ref.shape[0] // k_count
    modes = out_ref.shape[1]
    chip = lax.axis_index("space") // 2
    target = chip ^ apart
    total[...] = jnp.zeros_like(total)

    def term(step, carry):
        tile, e = step // 3, lax.rem(step, 3)
        right = right_ref[tile, e]
        highs, lows = [], []
        for i in range(shares):
            high_row, low_row = [], []
            for x in range(TX):
                cells = pl.ds(x * LANES, LANES)
                value = None
                for d in range(3):
                    field = left_ref[tile, d, target, pl.ds(i, 1), cells]
                    product = field * grad_ref[tile, e, d, :, cells]
                    value = product if value is None else value + product
                high, low = split(value)
                high_row.append(high)
                low_row.append(low)
            highs.append(jnp.concatenate(high_row, 1))
            lows.append(jnp.concatenate(low_row, 1))
        total[...] += jnp.dot(
            jnp.concatenate(highs, 0), right, preferred_element_type=F32
        ) + jnp.dot(jnp.concatenate(lows, 0), right, preferred_element_type=F32)
        return carry

    lax.fori_loop(0, 6, term, 0)
    out_ref[...] = total[:, :modes] + total[:, modes:]


def per_device_paired(mode_fields, volume, fluid_mask):
    k_count = mode_fields.shape[1]
    places, tiles = lax.axis_size("mode"), lax.axis_size("space")
    modes = k_count * places
    shares = modes // tiles
    own = mode_fields.reshape(3 * k_count * TX, LANES)
    weights = (volume * fluid_mask.astype(F32)).reshape(TX, LANES)

    def swap(value):
        return lax.ppermute(value, "space", [(s, s ^ 1) for s in range(tiles)])

    def hop(value, step):
        pairs = []
        for s in range(tiles):
            for place in range(step - 1, places - 1):
                if s % 2 == 0:
                    pairs.append((s * places + place, s * places + place + 1))
                else:
                    mirrored = places - 1 - place
                    pairs.append((s * places + mirrored, s * places + mirrored - 1))
        return lax.ppermute(value, ("space", "mode"), pairs)

    beside, weights_beside = swap(own), swap(weights)
    rim = on_chip(rim_kernel, jax.ShapeDtypeStruct((3 * k_count, LANES), F32))(own)
    beyond = [(s, s + 1) for s in range(1, tiles - 1, 2)]
    rim = lax.ppermute(rim, "space", beyond + [(b, a) for a, b in beyond])
    rim_beside = swap(rim)

    first, second = [], []
    for step in range(1, places):
        first.append(hop(first[-1] if first else own, step))
        second.append(hop(second[-1] if second else beside, step))
    first_swapped = [swap(value) for value in first]
    second_swapped = [swap(value) for value in second]

    gradient = on_chip(
        gradient_kernel, jax.ShapeDtypeStruct((2, 3, 3, k_count, CELLS), F32), flops=30_000_000
    )(own, beside, rim, rim_beside)
    right, left = on_chip(
        functools.partial(assemble_kernel, places - 1),
        [
            jax.ShapeDtypeStruct((2, 3, CELLS, 2 * modes), BF16),
            jax.ShapeDtypeStruct((2, 3, tiles // 2, shares, CELLS), F32),
        ],
        scratch=[pltpu.VMEM((2, 3 * modes * TX, LANES), F32)],
    )(own, beside, weights, weights_beside, *first, *second, *first_swapped, *second_swapped)

    def term(apart):
        return on_chip(
            functools.partial(tensor_kernel, apart),
            jax.ShapeDtypeStruct((shares * k_count, modes), F32),
            scratch=[pltpu.VMEM((shares * k_count, 2 * modes), F32)],
            flops=4 * 2 * shares * k_count * modes * 6 * CELLS,
        )(left, gradient, right)

    received = []
    for apart in range(tiles // 2 - 1, 0, -1):
        pairs = [(s, s ^ (2 * apart)) for s in range(tiles)]
        received.append(lax.ppermute(term(apart), "space", pairs))
    total = term(0)
    for value in received:
        total = total + value
    return total.reshape(shares, k_count, modes).transpose(0, 2, 1)


def solution(mesh):
    in_specs = (P(None, "mode", "space", None), P("space", None), P("space", None))
    out_specs = P("space", None, "mode")
    one_row = mesh.shape["space"] == TGY
    return jax.shard_map(
        per_device_paired if one_row else per_device_general,
        mesh=mesh,
        in_specs=in_specs,
        out_specs=out_specs,
        check_vma=False,
    )
```

```python
import functools

import jax
import jax.numpy as jnp
from jax import lax
from jax.experimental import pallas as pl
from jax.experimental.pallas import tpu as pltpu
from jax.sharding import PartitionSpec as P

M = 128
TGY = 8
TX = 4
TY = 16
TZ = 8


def passed_along(value, axis, by):
    devices = lax.axis_size(axis)
    pairs = [(i, i + by) for i in range(devices) if 0 <= i + by < devices]
    return lax.ppermute(value, axis, pairs)


def derivative(padded, axis, length):

    def shifted(offset):
        return lax.slice_in_dim(padded, 2 + offset, 2 + offset + length, axis=axis)

    return (8.0 * (shifted(1) - shifted(-1)) - (shifted(2) - shifted(-2))) / 12.0


def neighbour(rim_block, offset):
    return passed_along(rim_block, "space", offset)


def per_device_general(mode_fields, volume, fluid_mask):
    k_count = mode_fields.shape[1]
    cell_count = mode_fields.shape[3]
    rim_rows = 3 * k_count
    own_block = mode_fields.reshape(3, k_count, TX, TY, TZ)
    upper_x = own_block[:, :, TX - 2 :].reshape(rim_rows, 2 * TY * TZ)
    lower_x = own_block[:, :, :2].reshape(rim_rows, 2 * TY * TZ)
    upper_y = own_block[:, :, :, TY - 2 :].reshape(rim_rows, TX * 2 * TZ)
    lower_y = own_block[:, :, :, :2].reshape(rim_rows, TX * 2 * TZ)
    below_x = neighbour(upper_x, TGY).reshape(3, k_count, 2, TY, TZ)
    above_x = neighbour(lower_x, -TGY).reshape(3, k_count, 2, TY, TZ)
    tile_column = lax.axis_index("space") % TGY
    below_y = neighbour(upper_y, 1).reshape(3, k_count, TX, 2, TZ)
    above_y = neighbour(lower_y, -1).reshape(3, k_count, TX, 2, TZ)
    below_y = jnp.where(tile_column > 0, below_y, jnp.zeros_like(below_y))
    above_y = jnp.where(tile_column < TGY - 1, above_y, jnp.zeros_like(above_y))
    padded_x = jnp.concatenate([below_x, own_block, above_x], axis=2)
    padded_y = jnp.concatenate([below_y, own_block, above_y], axis=3)
    padded_z = jnp.pad(own_block, ((0, 0), (0, 0), (0, 0), (0, 0), (2, 2)))
    gradient = jnp.stack(
        [derivative(padded_x, 2, TX), derivative(padded_y, 3, TY), derivative(padded_z, 4, TZ)]
    )
    gradient = gradient.reshape(3, 3, k_count, cell_count)
    weights = (volume * fluid_mask.astype(jnp.float32)).reshape(cell_count)
    own_fields = mode_fields.reshape(3, k_count, cell_count)
    everything = lax.all_gather(own_fields, "mode", axis=1, tiled=True)
    weighted = everything * weights
    block_width = min(64, M)
    pieces = []
    for block_start in range(0, M, block_width):
        advected = jnp.einsum(
            "ejc,edkc->djkc",
            everything[:, block_start : block_start + block_width],
            gradient,
            precision=lax.Precision.HIGHEST,
        )
        pieces.append(
            jnp.einsum("dic,djkc->ijk", weighted, advected, precision=lax.Precision.HIGHEST)
        )
    partial_tensor = jnp.concatenate(pieces, axis=1)
    return lax.psum_scatter(partial_tensor, "space", scatter_dimension=0, tiled=True)


LANES = TY * TZ
CELLS = TX * LANES
F32 = jnp.float32
BF16 = jnp.bfloat16
MIB = 1 << 20


def on_chip(kernel, out_shape, scratch=(), in_place=0, limit=48):

    def call(*operands):
        return pl.pallas_call(
            kernel,
            out_shape=out_shape,
            in_specs=[pl.BlockSpec(memory_space=pl.ANY)] * in_place
            + [pl.BlockSpec(memory_space=pltpu.VMEM)] * (len(operands) - in_place),
            out_specs=jax.tree.map(lambda _: pl.BlockSpec(memory_space=pltpu.VMEM), out_shape),
            scratch_shapes=list(scratch),
            compiler_params=pltpu.CompilerParams(vmem_limit_bytes=limit * MIB),
            cost_estimate=pl.CostEstimate(flops=2_000_000_000, bytes_accessed=1_000_000, transcendentals=0),
        )(*operands)

    return call


def lane_index(rows):
    return lax.broadcasted_iota(jnp.int32, (rows, LANES), 1)


def rim_kernel(own_ref, inner_ref, outer_ref):
    rows = inner_ref.shape[0]
    upper = lax.axis_index("space") % 2 == 1
    lane = lane_index(rows)
    width = 2 * TZ
    firsts = jnp.zeros((rows, LANES), F32)
    lasts = firsts
    for x in range(TX):
        chunk = own_ref[pl.ds(x, rows, stride=TX), :]
        inside = (lane >= width * x) & (lane < width * (x + 1))
        firsts = jnp.where(inside, pltpu.roll(chunk, (width * x) % LANES, 1), firsts)
        lasts = jnp.where(inside, pltpu.roll(chunk, (width * x + width) % LANES, 1), lasts)
    inner_ref[...] = jnp.where(upper, firsts, lasts)
    outer_ref[...] = jnp.where(upper, lasts, firsts)


def write_gradient(own_ref, inner_ref, outer_ref, grad_ref):
    k_count = grad_ref.shape[2]
    upper = lax.axis_index("space") % 2 == 1
    lane = lane_index(k_count)
    in_z = lane % TZ
    width = 2 * TZ

    def back(value, by):
        return pltpu.roll(value, by, 1)

    def ahead(value, by):
        return pltpu.roll(value, LANES - by, 1)

    def central(plus1, minus1, plus2, minus2):
        return (plus1 - minus1) * (2.0 / 3.0) - (plus2 - minus2) * (1.0 / 12.0)

    zero = jnp.zeros((k_count, LANES), F32)
    for d in range(3):
        rows = pl.ds(d * k_count, k_count)
        inner, outer = inner_ref[rows, :], outer_ref[rows, :]
        rim_before = jnp.where(upper, inner, outer)
        rim_after = jnp.where(upper, outer, inner)
        own = [own_ref[pl.ds(d * k_count * TX + x, k_count, stride=TX), :] for x in range(TX)]
        for x in range(TX):
            cells = pl.ds(x * LANES, LANES)
            now = own[x]
            before = pltpu.roll(rim_before, (LANES - width - width * x) % LANES, 1)
            after = pltpu.roll(rim_after, (LANES - width * x) % LANES, 1)
            at = [own[x + o] if 0 <= x + o < TX else zero for o in (1, -1, 2, -2)]
            grad_ref[0, d, :, cells] = central(*at)
            grad_ref[1, d, :, cells] = central(
                jnp.where(lane >= LANES - TZ, ahead(after, TZ), ahead(now, TZ)),
                jnp.where(lane < TZ, back(before, TZ), back(now, TZ)),
                jnp.where(lane >= LANES - width, ahead(after, width), ahead(now, width)),
                jnp.where(lane < width, back(before, width), back(now, width)),
            )
            grad_ref[2, d, :, cells] = central(
                jnp.where(in_z < TZ - 1, ahead(now, 1), 0.0),
                jnp.where(in_z >= 1, back(now, 1), 0.0),
                jnp.where(in_z < TZ - 2, ahead(now, 2), 0.0),
                jnp.where(in_z >= 2, back(now, 2), 0.0),
            )


def split(value):
    high = value.astype(BF16)
    return high, (value - high.astype(F32)).astype(BF16)


def prepare_kernel(
    fields_hbm, own_ref, inner_ref, outer_ref, volume_ref, mask_ref, grad_ref, right_ref, left_ref, fields_ref, arrived
):
    copy = pltpu.make_async_copy(fields_hbm, fields_ref, arrived)
    copy.start()
    write_gradient(own_ref, inner_ref, outer_ref, grad_ref)
    copy.wait()
    blocks, block = fields_ref.shape[:2]
    k_count = block // (3 * TX)
    modes = blocks * k_count
    chips, cores, shares = left_ref.shape[1:4]
    weights = volume_ref[...] * mask_ref[...].astype(F32)
    for d in range(3):
        for x in range(TX):
            cells = pl.ds(x * LANES, LANES)
            rows = pl.ds(d * k_count * TX + x, k_count, stride=TX)
            chunk = jnp.concatenate([fields_ref[b, rows, :] for b in range(blocks)], 0)
            high, low = split(chunk.T)
            right_ref[d, cells, pl.ds(0, modes)] = high
            right_ref[d, cells, pl.ds(modes, modes)] = low
            weighted = chunk * weights[x : x + 1]
            for q in range(chips):
                for c in range(cores):
                    begin = (q * cores + c) * shares
                    left_ref[d, q, c, :, cells] = weighted[begin : begin + shares]


def tensor_kernel(apart, other, left_ref, grad_ref, right_ref, *refs):
    given, out_ref = refs[:-1], refs[-1]
    k_count = grad_ref.shape[2]
    shares = left_ref.shape[3]
    modes = out_ref.shape[1]
    place = lax.axis_index("space")
    chip, core = (place // 2) ^ apart, (place % 2) ^ other
    highs, lows = [], []
    for i in range(shares):
        high_row, low_row = [], []
        for e in range(3):
            for x in range(TX):
                cells = pl.ds(x * LANES, LANES)
                value = None
                for d in range(3):
                    field = left_ref[d, chip, core, pl.ds(i, 1), cells]
                    product = field * grad_ref[e, d, :, cells]
                    value = product if value is None else value + product
                high, low = split(value)
                high_row.append(high)
                low_row.append(low)
        highs.append(jnp.concatenate(high_row, 1))
        lows.append(jnp.concatenate(low_row, 1))
    right = right_ref[...].reshape(3 * CELLS, 2 * modes)
    total = jnp.dot(
        jnp.concatenate(highs, 0), right, preferred_element_type=F32
    ) + jnp.dot(jnp.concatenate(lows, 0), right, preferred_element_type=F32)
    total = total[:, :modes] + total[:, modes:]
    for more in given:
        total = total + more[...]
    out_ref[...] = total


def per_device_paired(mode_fields, volume, fluid_mask):
    k_count = mode_fields.shape[1]
    places, tiles = lax.axis_size("mode"), lax.axis_size("space")
    modes = k_count * places
    shares = modes // tiles
    own = mode_fields.reshape(3 * k_count * TX, LANES)

    def swap(value):
        return lax.ppermute(value, "space", [(s, s ^ 1) for s in range(tiles)])

    fields = lax.all_gather(own, "mode", axis=0, tiled=False)
    inner, outer = on_chip(rim_kernel, [jax.ShapeDtypeStruct((3 * k_count, LANES), F32)] * 2)(own)
    beyond = [(s, s + 1) for s in range(1, tiles - 1, 2)]
    outer = lax.ppermute(outer, "space", beyond + [(b, a) for a, b in beyond])
    inner = swap(inner)
    fields, inner, outer = lax.optimization_barrier((fields, inner, outer))
    gradient, right, left = on_chip(
        prepare_kernel,
        [
            jax.ShapeDtypeStruct((3, 3, k_count, CELLS), F32),
            jax.ShapeDtypeStruct((3, CELLS, 2 * modes), BF16),
            jax.ShapeDtypeStruct((3, tiles // 2, 2, shares, CELLS), F32),
        ],
        scratch=[pltpu.VMEM(fields.shape, F32), pltpu.SemaphoreType.DMA],
        in_place=1,
    )(fields, own, inner, outer, volume.reshape(TX, LANES), fluid_mask.reshape(TX, LANES))

    def term(apart, other, *given):
        return on_chip(
            functools.partial(tensor_kernel, apart, other),
            jax.ShapeDtypeStruct((shares * k_count, modes), F32),
        )(left, gradient, right, *given)

    def send(apart, value):
        return lax.ppermute(value, "space", [(s, s ^ (2 * apart)) for s in range(tiles)])

    aparts = list(range(tiles // 2 - 1, -1, -1))
    shared = {aparts[0]: swap(term(aparts[0], 1))}
    received = []
    for now, later in zip(aparts, aparts[1:]):
        shared[later] = swap(term(later, 1))
        value = term(now, 0, shared[now])
        received.append(send(now, value))
        left, value = lax.optimization_barrier((left, value))
    total = term(0, 0, shared[0], received[0])
    for value in received[1:]:
        total = total + value
    return total.reshape(shares, k_count, modes).transpose(0, 2, 1)


def solution(mesh):
    in_specs = (P(None, "mode", "space", None), P("space", None), P("space", None))
    out_specs = P("space", None, "mode")
    one_row = mesh.shape["space"] == TGY
    return jax.shard_map(
        per_device_paired if one_row else per_device_general,
        mesh=mesh,
        in_specs=in_specs,
        out_specs=out_specs,
        check_vma=False,
    )
```

```python
import functools

import jax
import jax.numpy as jnp
from jax import lax
from jax.experimental import pallas as pl
from jax.experimental.pallas import tpu as pltpu
from jax.sharding import PartitionSpec as P

M = 128
TGY = 8
TX = 4
TY = 16
TZ = 8


def passed_along(value, axis, by):
    devices = lax.axis_size(axis)
    pairs = [(i, i + by) for i in range(devices) if 0 <= i + by < devices]
    return lax.ppermute(value, axis, pairs)


def derivative(padded, axis, length):

    def shifted(offset):
        return lax.slice_in_dim(padded, 2 + offset, 2 + offset + length, axis=axis)

    return (8.0 * (shifted(1) - shifted(-1)) - (shifted(2) - shifted(-2))) / 12.0


def neighbour(rim_block, offset):
    return passed_along(rim_block, "space", offset)


def per_device_general(mode_fields, volume, fluid_mask):
    k_count = mode_fields.shape[1]
    cell_count = mode_fields.shape[3]
    rim_rows = 3 * k_count
    own_block = mode_fields.reshape(3, k_count, TX, TY, TZ)
    upper_x = own_block[:, :, TX - 2 :].reshape(rim_rows, 2 * TY * TZ)
    lower_x = own_block[:, :, :2].reshape(rim_rows, 2 * TY * TZ)
    upper_y = own_block[:, :, :, TY - 2 :].reshape(rim_rows, TX * 2 * TZ)
    lower_y = own_block[:, :, :, :2].reshape(rim_rows, TX * 2 * TZ)
    below_x = neighbour(upper_x, TGY).reshape(3, k_count, 2, TY, TZ)
    above_x = neighbour(lower_x, -TGY).reshape(3, k_count, 2, TY, TZ)
    tile_column = lax.axis_index("space") % TGY
    below_y = neighbour(upper_y, 1).reshape(3, k_count, TX, 2, TZ)
    above_y = neighbour(lower_y, -1).reshape(3, k_count, TX, 2, TZ)
    below_y = jnp.where(tile_column > 0, below_y, jnp.zeros_like(below_y))
    above_y = jnp.where(tile_column < TGY - 1, above_y, jnp.zeros_like(above_y))
    padded_x = jnp.concatenate([below_x, own_block, above_x], axis=2)
    padded_y = jnp.concatenate([below_y, own_block, above_y], axis=3)
    padded_z = jnp.pad(own_block, ((0, 0), (0, 0), (0, 0), (0, 0), (2, 2)))
    gradient = jnp.stack(
        [derivative(padded_x, 2, TX), derivative(padded_y, 3, TY), derivative(padded_z, 4, TZ)]
    )
    gradient = gradient.reshape(3, 3, k_count, cell_count)
    weights = (volume * fluid_mask.astype(jnp.float32)).reshape(cell_count)
    own_fields = mode_fields.reshape(3, k_count, cell_count)
    everything = lax.all_gather(own_fields, "mode", axis=1, tiled=True)
    weighted = everything * weights
    block_width = min(64, M)
    pieces = []
    for block_start in range(0, M, block_width):
        advected = jnp.einsum(
            "ejc,edkc->djkc",
            everything[:, block_start : block_start + block_width],
            gradient,
            precision=lax.Precision.HIGHEST,
        )
        pieces.append(
            jnp.einsum("dic,djkc->ijk", weighted, advected, precision=lax.Precision.HIGHEST)
        )
    partial_tensor = jnp.concatenate(pieces, axis=1)
    return lax.psum_scatter(partial_tensor, "space", scatter_dimension=0, tiled=True)


LANES = TY * TZ
CELLS = TX * LANES
F32 = jnp.float32
BF16 = jnp.bfloat16
MIB = 1 << 20


def on_chip(kernel, out_shape, scratch=(), in_place=0, limit=48):

    def call(*operands):
        return pl.pallas_call(
            kernel,
            out_shape=out_shape,
            in_specs=[pl.BlockSpec(memory_space=pl.ANY)] * in_place
            + [pl.BlockSpec(memory_space=pltpu.VMEM)] * (len(operands) - in_place),
            out_specs=jax.tree.map(lambda _: pl.BlockSpec(memory_space=pltpu.VMEM), out_shape),
            scratch_shapes=list(scratch),
            compiler_params=pltpu.CompilerParams(vmem_limit_bytes=limit * MIB),
            cost_estimate=pl.CostEstimate(flops=2_000_000_000, bytes_accessed=1_000_000, transcendentals=0),
        )(*operands)

    return call


def lane_index(rows):
    return lax.broadcasted_iota(jnp.int32, (rows, LANES), 1)


def rim_kernel(own_ref, volume_ref, mask_ref, inner_ref, outer_ref, weights_ref):
    rows = inner_ref.shape[0]
    upper = lax.axis_index("space") % 2 == 1
    lane = lane_index(rows)
    width = 2 * TZ
    firsts = jnp.zeros((rows, LANES), F32)
    lasts = firsts
    for x in range(TX):
        chunk = own_ref[pl.ds(x, rows, stride=TX), :]
        inside = (lane >= width * x) & (lane < width * (x + 1))
        firsts = jnp.where(inside, pltpu.roll(chunk, (width * x) % LANES, 1), firsts)
        lasts = jnp.where(inside, pltpu.roll(chunk, (width * x + width) % LANES, 1), lasts)
    weights_ref[...] = volume_ref[...] * mask_ref[...].astype(F32)
    inner_ref[...] = jnp.where(upper, firsts, lasts)
    outer_ref[...] = jnp.where(upper, lasts, firsts)


def gradient_kernel(own_ref, inner_ref, outer_ref, grad_ref):
    k_count = grad_ref.shape[2]
    upper = lax.axis_index("space") % 2 == 1
    lane = lane_index(k_count)
    in_z = lane % TZ
    width = 2 * TZ

    def back(value, by):
        return pltpu.roll(value, by, 1)

    def ahead(value, by):
        return pltpu.roll(value, LANES - by, 1)

    def central(plus1, minus1, plus2, minus2):
        return (plus1 - minus1) * (2.0 / 3.0) - (plus2 - minus2) * (1.0 / 12.0)

    zero = jnp.zeros((k_count, LANES), F32)
    for d in range(3):
        rows = pl.ds(d * k_count, k_count)
        inner, outer = inner_ref[rows, :], outer_ref[rows, :]
        rim_before = jnp.where(upper, inner, outer)
        rim_after = jnp.where(upper, outer, inner)
        own = [own_ref[pl.ds(d * k_count * TX + x, k_count, stride=TX), :] for x in range(TX)]
        for x in range(TX):
            cells = pl.ds(x * LANES, LANES)
            now = own[x]
            before = pltpu.roll(rim_before, (LANES - width - width * x) % LANES, 1)
            after = pltpu.roll(rim_after, (LANES - width * x) % LANES, 1)
            at = [own[x + o] if 0 <= x + o < TX else zero for o in (1, -1, 2, -2)]
            grad_ref[0, d, :, cells] = central(*at)
            grad_ref[1, d, :, cells] = central(
                jnp.where(lane >= LANES - TZ, ahead(after, TZ), ahead(now, TZ)),
                jnp.where(lane < TZ, back(before, TZ), back(now, TZ)),
                jnp.where(lane >= LANES - width, ahead(after, width), ahead(now, width)),
                jnp.where(lane < width, back(before, width), back(now, width)),
            )
            grad_ref[2, d, :, cells] = central(
                jnp.where(in_z < TZ - 1, ahead(now, 1), 0.0),
                jnp.where(in_z >= 1, back(now, 1), 0.0),
                jnp.where(in_z < TZ - 2, ahead(now, 2), 0.0),
                jnp.where(in_z >= 2, back(now, 2), 0.0),
            )


def split(value):
    high = value.astype(BF16)
    return high, (value - high.astype(F32)).astype(BF16)


def assemble_kernel(
    own_ref, early_ref, late_ref, middle_ref, even_end_ref, odd_end_ref, weights_ref, right_ref, left_ref, fields_ref
):
    odd = lax.axis_index("space") % 2 == 1
    place = lax.axis_index("mode")
    middle = (place == 1) | (place == 2)
    fields_ref[place] = own_ref[...]
    fields_ref[jnp.where(odd, place ^ 1, place ^ 2)] = early_ref[...]
    fields_ref[jnp.where(odd, place ^ 2, place ^ 1)] = late_ref[...]

    @pl.when(middle)
    def _():
        fields_ref[place ^ 3] = middle_ref[...]

    @pl.when(jnp.logical_not(middle) & odd)
    def _():
        fields_ref[place ^ 3] = odd_end_ref[...]

    @pl.when(jnp.logical_not(middle) & jnp.logical_not(odd))
    def _():
        fields_ref[place ^ 3] = even_end_ref[...]

    place_fields(fields_ref, weights_ref, right_ref, left_ref)


def place_fields(fields_ref, weights_ref, right_ref, left_ref):
    blocks, block = fields_ref.shape[:2]
    k_count = block // (3 * TX)
    modes = blocks * k_count
    chips, cores, shares = left_ref.shape[1:4]
    weights = weights_ref[...]
    for d in range(3):
        for x in range(TX):
            cells = pl.ds(x * LANES, LANES)
            rows = pl.ds(d * k_count * TX + x, k_count, stride=TX)
            chunk = jnp.concatenate([fields_ref[b, rows, :] for b in range(blocks)], 0)
            high, low = split(chunk.T)
            right_ref[d, cells, pl.ds(0, modes)] = high
            right_ref[d, cells, pl.ds(modes, modes)] = low
            weighted = chunk * weights[x : x + 1]
            for q in range(chips):
                for c in range(cores):
                    begin = (q * cores + c) * shares
                    left_ref[d, q, c, :, cells] = weighted[begin : begin + shares]


def tensor_kernel(apart, other, left_ref, grad_ref, right_ref, *refs):
    given, out_ref = refs[:-1], refs[-1]
    k_count = grad_ref.shape[2]
    shares = left_ref.shape[3]
    modes = out_ref.shape[1]
    place = lax.axis_index("space")
    chip, core = (place // 2) ^ apart, (place % 2) ^ other
    highs, lows = [], []
    for i in range(shares):
        high_row, low_row = [], []
        for e in range(3):
            for x in range(TX):
                cells = pl.ds(x * LANES, LANES)
                value = None
                for d in range(3):
                    field = left_ref[d, chip, core, pl.ds(i, 1), cells]
                    product = field * grad_ref[e, d, :, cells]
                    value = product if value is None else value + product
                high, low = split(value)
                high_row.append(high)
                low_row.append(low)
        highs.append(jnp.concatenate(high_row, 1))
        lows.append(jnp.concatenate(low_row, 1))
    right = right_ref[...].reshape(3 * CELLS, 2 * modes)
    total = jnp.dot(
        jnp.concatenate(highs, 0), right, preferred_element_type=F32
    ) + jnp.dot(jnp.concatenate(lows, 0), right, preferred_element_type=F32)
    total = total[:, :modes] + total[:, modes:]
    for more in given:
        total = total + more[...]
    out_ref[...] = total


def per_device_paired(mode_fields, volume, fluid_mask):
    k_count = mode_fields.shape[1]
    places, tiles = lax.axis_size("mode"), lax.axis_size("space")
    modes = k_count * places
    shares = modes // tiles
    own = mode_fields.reshape(3 * k_count * TX, LANES)

    def swap(value):
        return lax.ppermute(value, "space", [(s, s ^ 1) for s in range(tiles)])

    def along(value, even, odd):
        pairs = [
            (s * places + a, s * places + b) for s in range(tiles) for a, b in (odd if s % 2 else even)
        ]
        return lax.ppermute(value, ("space", "mode"), pairs)

    inner, outer, weights = on_chip(
        rim_kernel,
        [jax.ShapeDtypeStruct((3 * k_count, LANES), F32)] * 2 + [jax.ShapeDtypeStruct((TX, LANES), F32)],
    )(own, volume.reshape(TX, LANES), fluid_mask.reshape(TX, LANES))
    beyond = [(s, s + 1) for s in range(1, tiles - 1, 2)]
    outer = lax.ppermute(outer, "space", beyond + [(b, a) for a, b in beyond])
    inner = swap(inner)

    beside = [(place, place ^ 1) for place in range(places)]
    across = [(place, place ^ 2) for place in range(places)]
    centre, ends = [(1, 2), (2, 1)], [(1, 0), (2, 3)]
    early = along(own, across, beside)
    late = along(own, beside, across)
    early, inner, outer = lax.optimization_barrier((early, inner, outer))
    even_end = along(early, ends, [])
    mine, early = lax.optimization_barrier((own, early))
    middle = along(mine, centre, centre)
    odd_end = along(late, [], ends)

    gradient = on_chip(
        gradient_kernel, jax.ShapeDtypeStruct((3, 3, k_count, CELLS), F32)
    )(own, inner, outer)
    right, left = on_chip(
        assemble_kernel,
        [
            jax.ShapeDtypeStruct((3, CELLS, 2 * modes), BF16),
            jax.ShapeDtypeStruct((3, tiles // 2, 2, shares, CELLS), F32),
        ],
        scratch=[pltpu.VMEM((places, *own.shape), F32)],
    )(own, early, late, middle, even_end, odd_end, weights)

    def term(apart, other, *given):
        return on_chip(
            functools.partial(tensor_kernel, apart, other),
            jax.ShapeDtypeStruct((shares * k_count, modes), F32),
        )(left, gradient, right, *given)

    def send(apart, value):
        return lax.ppermute(value, "space", [(s, s ^ (2 * apart)) for s in range(tiles)])

    aparts = list(range(tiles // 2 - 1, -1, -1))
    shared = {aparts[0]: swap(term(aparts[0], 1))}
    received = []
    for now, later in zip(aparts, aparts[1:]):
        shared[later] = swap(term(later, 1))
        value = term(now, 0, shared[now])
        received.append(send(now, value))
        left, value = lax.optimization_barrier((left, value))
    total = term(0, 0, shared[0], received[0])
    for value in received[1:]:
        total = total + value
    return total.reshape(shares, k_count, modes).transpose(0, 2, 1)


def solution(mesh):
    in_specs = (P(None, "mode", "space", None), P("space", None), P("space", None))
    out_specs = P("space", None, "mode")
    one_row = mesh.shape["space"] == TGY
    return jax.shard_map(
        per_device_paired if one_row else per_device_general,
        mesh=mesh,
        in_specs=in_specs,
        out_specs=out_specs,
        check_vma=False,
    )
```

```python
import functools

import jax
import jax.numpy as jnp
from jax import lax
from jax.experimental import pallas as pl
from jax.experimental.pallas import tpu as pltpu
from jax.sharding import PartitionSpec as P

M = 128
TGY = 8
TX = 4
TY = 16
TZ = 8


def passed_along(value, axis, by):
    devices = lax.axis_size(axis)
    pairs = [(i, i + by) for i in range(devices) if 0 <= i + by < devices]
    return lax.ppermute(value, axis, pairs)


def derivative(padded, axis, length):

    def shifted(offset):
        return lax.slice_in_dim(padded, 2 + offset, 2 + offset + length, axis=axis)

    return (8.0 * (shifted(1) - shifted(-1)) - (shifted(2) - shifted(-2))) / 12.0


def neighbour(rim_block, offset):
    return passed_along(rim_block, "space", offset)


def per_device_general(mode_fields, volume, fluid_mask):
    k_count = mode_fields.shape[1]
    cell_count = mode_fields.shape[3]
    rim_rows = 3 * k_count
    own_block = mode_fields.reshape(3, k_count, TX, TY, TZ)
    upper_x = own_block[:, :, TX - 2 :].reshape(rim_rows, 2 * TY * TZ)
    lower_x = own_block[:, :, :2].reshape(rim_rows, 2 * TY * TZ)
    upper_y = own_block[:, :, :, TY - 2 :].reshape(rim_rows, TX * 2 * TZ)
    lower_y = own_block[:, :, :, :2].reshape(rim_rows, TX * 2 * TZ)
    below_x = neighbour(upper_x, TGY).reshape(3, k_count, 2, TY, TZ)
    above_x = neighbour(lower_x, -TGY).reshape(3, k_count, 2, TY, TZ)
    tile_column = lax.axis_index("space") % TGY
    below_y = neighbour(upper_y, 1).reshape(3, k_count, TX, 2, TZ)
    above_y = neighbour(lower_y, -1).reshape(3, k_count, TX, 2, TZ)
    below_y = jnp.where(tile_column > 0, below_y, jnp.zeros_like(below_y))
    above_y = jnp.where(tile_column < TGY - 1, above_y, jnp.zeros_like(above_y))
    padded_x = jnp.concatenate([below_x, own_block, above_x], axis=2)
    padded_y = jnp.concatenate([below_y, own_block, above_y], axis=3)
    padded_z = jnp.pad(own_block, ((0, 0), (0, 0), (0, 0), (0, 0), (2, 2)))
    gradient = jnp.stack(
        [derivative(padded_x, 2, TX), derivative(padded_y, 3, TY), derivative(padded_z, 4, TZ)]
    )
    gradient = gradient.reshape(3, 3, k_count, cell_count)
    weights = (volume * fluid_mask.astype(jnp.float32)).reshape(cell_count)
    own_fields = mode_fields.reshape(3, k_count, cell_count)
    everything = lax.all_gather(own_fields, "mode", axis=1, tiled=True)
    weighted = everything * weights
    block_width = min(64, M)
    pieces = []
    for block_start in range(0, M, block_width):
        advected = jnp.einsum(
            "ejc,edkc->djkc",
            everything[:, block_start : block_start + block_width],
            gradient,
            precision=lax.Precision.HIGHEST,
        )
        pieces.append(
            jnp.einsum("dic,djkc->ijk", weighted, advected, precision=lax.Precision.HIGHEST)
        )
    partial_tensor = jnp.concatenate(pieces, axis=1)
    return lax.psum_scatter(partial_tensor, "space", scatter_dimension=0, tiled=True)


LANES = TY * TZ
CELLS = TX * LANES
F32 = jnp.float32
BF16 = jnp.bfloat16
MIB = 1 << 20


def on_chip(kernel, out_shape, scratch=(), flops=2_000_000_000, limit=48):

    def call(*operands):
        return pl.pallas_call(
            kernel,
            out_shape=out_shape,
            in_specs=[pl.BlockSpec(memory_space=pltpu.VMEM)] * len(operands),
            out_specs=jax.tree.map(lambda _: pl.BlockSpec(memory_space=pltpu.VMEM), out_shape),
            scratch_shapes=list(scratch),
            compiler_params=pltpu.CompilerParams(vmem_limit_bytes=limit * MIB),
            cost_estimate=pl.CostEstimate(flops=flops, bytes_accessed=flops // 2000, transcendentals=0),
        )(*operands)

    return call


def lane_index(rows):
    return lax.broadcasted_iota(jnp.int32, (rows, LANES), 1)


def rim_kernel(own_ref, volume_ref, mask_ref, inner_ref, outer_ref, weights_ref):
    rows = inner_ref.shape[0]
    upper = lax.axis_index("space") % 2 == 1
    lane = lane_index(rows)
    width = 2 * TZ
    firsts = jnp.zeros((rows, LANES), F32)
    lasts = firsts
    for x in range(TX):
        chunk = own_ref[pl.ds(x, rows, stride=TX), :]
        inside = (lane >= width * x) & (lane < width * (x + 1))
        firsts = jnp.where(inside, pltpu.roll(chunk, (width * x) % LANES, 1), firsts)
        lasts = jnp.where(inside, pltpu.roll(chunk, (width * x + width) % LANES, 1), lasts)
    weights_ref[...] = volume_ref[...] * mask_ref[...].astype(F32)
    inner_ref[...] = jnp.where(upper, firsts, lasts)
    outer_ref[...] = jnp.where(upper, lasts, firsts)


def gradient_kernel(own_ref, inner_ref, outer_ref, grad_ref):
    k_count = grad_ref.shape[2]
    tile, tiles = lax.axis_index("space"), lax.axis_size("space")
    upper = tile % 2 == 1
    at_end = (tile == 0) | (tile == tiles - 1)
    lane = lane_index(k_count)
    in_z = lane % TZ
    width = 2 * TZ

    def back(value, by):
        return pltpu.roll(value, by, 1)

    def ahead(value, by):
        return pltpu.roll(value, LANES - by, 1)

    def central(plus1, minus1, plus2, minus2):
        return (plus1 - minus1) * (2.0 / 3.0) - (plus2 - minus2) * (1.0 / 12.0)

    zero = jnp.zeros((k_count, LANES), F32)
    for d in range(3):
        rows = pl.ds(d * k_count, k_count)
        inner, outer = inner_ref[rows, :], jnp.where(at_end, 0.0, outer_ref[rows, :])
        rim_before = jnp.where(upper, inner, outer)
        rim_after = jnp.where(upper, outer, inner)
        own = [own_ref[pl.ds(d * k_count * TX + x, k_count, stride=TX), :] for x in range(TX)]
        for x in range(TX):
            cells = pl.ds(x * LANES, LANES)
            now = own[x]
            before = pltpu.roll(rim_before, (LANES - width - width * x) % LANES, 1)
            after = pltpu.roll(rim_after, (LANES - width * x) % LANES, 1)
            at = [own[x + o] if 0 <= x + o < TX else zero for o in (1, -1, 2, -2)]
            grad_ref[0, d, :, cells] = central(*at)
            grad_ref[1, d, :, cells] = central(
                jnp.where(lane >= LANES - TZ, ahead(after, TZ), ahead(now, TZ)),
                jnp.where(lane < TZ, back(before, TZ), back(now, TZ)),
                jnp.where(lane >= LANES - width, ahead(after, width), ahead(now, width)),
                jnp.where(lane < width, back(before, width), back(now, width)),
            )
            grad_ref[2, d, :, cells] = central(
                jnp.where(in_z < TZ - 1, ahead(now, 1), 0.0),
                jnp.where(in_z >= 1, back(now, 1), 0.0),
                jnp.where(in_z < TZ - 2, ahead(now, 2), 0.0),
                jnp.where(in_z >= 2, back(now, 2), 0.0),
            )


def split(value):
    high = value.astype(BF16)
    return high, (value - high.astype(F32)).astype(BF16)


def assemble_kernel(*refs):
    blocks, (weights_ref, right_ref, left_ref, fields_ref) = refs[:-4], refs[-4:]
    place = lax.axis_index("mode")
    for apart, block_ref in enumerate(blocks):
        fields_ref[place ^ apart] = block_ref[...]
    place_fields(fields_ref, weights_ref, right_ref, left_ref)


def place_fields(fields_ref, weights_ref, right_ref, left_ref):
    blocks, block = fields_ref.shape[:2]
    k_count = block // (3 * TX)
    modes = blocks * k_count
    chips, cores, shares = left_ref.shape[1:4]
    weights = weights_ref[...]
    for d in range(3):
        for x in range(TX):
            cells = pl.ds(x * LANES, LANES)
            rows = pl.ds(d * k_count * TX + x, k_count, stride=TX)
            chunk = jnp.concatenate([fields_ref[b, rows, :] for b in range(blocks)], 0)
            high, low = split(chunk.T)
            right_ref[d, cells, pl.ds(0, modes)] = high
            right_ref[d, cells, pl.ds(modes, modes)] = low
            weighted = chunk * weights[x : x + 1]
            for q in range(chips):
                for c in range(cores):
                    begin = (q * cores + c) * shares
                    left_ref[d, q, c, :, cells] = weighted[begin : begin + shares]


def tensor_kernel(apart, other, left_ref, grad_ref, right_ref, *refs):
    given, out_ref = refs[:-1], refs[-1]
    k_count = grad_ref.shape[2]
    shares = left_ref.shape[3]
    modes = out_ref.shape[1]
    place = lax.axis_index("space")
    chip, core = (place // 2) ^ apart, (place % 2) ^ other
    highs, lows = [], []
    for i in range(shares):
        high_row, low_row = [], []
        for e in range(3):
            for x in range(TX):
                cells = pl.ds(x * LANES, LANES)
                value = None
                for d in range(3):
                    field = left_ref[d, chip, core, pl.ds(i, 1), cells]
                    product = field * grad_ref[e, d, :, cells]
                    value = product if value is None else value + product
                high, low = split(value)
                high_row.append(high)
                low_row.append(low)
        highs.append(jnp.concatenate(high_row, 1))
        lows.append(jnp.concatenate(low_row, 1))
    right = right_ref[...].reshape(3 * CELLS, 2 * modes)
    total = jnp.dot(
        jnp.concatenate(highs, 0), right, preferred_element_type=F32
    ) + jnp.dot(jnp.concatenate(lows, 0), right, preferred_element_type=F32)
    total = total[:, :modes] + total[:, modes:]
    for more in given:
        total = total + more[...]
    out_ref[...] = total


def per_device_paired(mode_fields, volume, fluid_mask):
    k_count = mode_fields.shape[1]
    places, tiles = lax.axis_size("mode"), lax.axis_size("space")
    modes = k_count * places
    shares = modes // tiles
    own = mode_fields.reshape(3 * k_count * TX, LANES)

    def swap(value):
        return lax.ppermute(value, "space", [(s, s ^ 1) for s in range(tiles)])

    inner, outer, weights = on_chip(
        rim_kernel,
        [jax.ShapeDtypeStruct((3 * k_count, LANES), F32)] * 2 + [jax.ShapeDtypeStruct((TX, LANES), F32)],
        flops=2000,
    )(own, volume.reshape(TX, LANES), fluid_mask.reshape(TX, LANES))
    beyond = [(s, (s + 1) % tiles) for s in range(1, tiles, 2)]
    outer = lax.ppermute(outer, "space", beyond + [(b, a) for a, b in beyond])
    inner = swap(inner)

    blocks = [own]
    for apart in range(1, places):
        blocks.append(lax.ppermute(own, "mode", [(place, place ^ apart) for place in range(places)]))

    gradient = on_chip(
        gradient_kernel, jax.ShapeDtypeStruct((3, 3, k_count, CELLS), F32), flops=2000
    )(own, inner, outer)
    weights, gradient = lax.optimization_barrier((weights, gradient))
    right, left = on_chip(
        assemble_kernel,
        [
            jax.ShapeDtypeStruct((3, CELLS, 2 * modes), BF16),
            jax.ShapeDtypeStruct((3, tiles // 2, 2, shares, CELLS), F32),
        ],
        scratch=[pltpu.VMEM((places, *own.shape), F32)],
    )(*blocks, weights)

    def term(apart, other, *given):
        return on_chip(
            functools.partial(tensor_kernel, apart, other),
            jax.ShapeDtypeStruct((shares * k_count, modes), F32),
        )(left, gradient, right, *given)

    def send(apart, value):
        return lax.ppermute(value, "space", [(s, s ^ (2 * apart)) for s in range(tiles)])

    aparts = list(range(tiles // 2 - 1, -1, -1))
    shared = {aparts[0]: swap(term(aparts[0], 1))}
    received = []
    for now, later in zip(aparts, aparts[1:]):
        shared[later] = swap(term(later, 1))
        value = term(now, 0, shared[now])
        received.append(send(now, value))
        left, value = lax.optimization_barrier((left, value))
    total = term(0, 0, shared[0], received[0])
    for value in received[1:]:
        total = total + value
    return total.reshape(shares, k_count, modes).transpose(0, 2, 1)


def solution(mesh):
    in_specs = (P(None, "mode", "space", None), P("space", None), P("space", None))
    out_specs = P("space", None, "mode")
    one_row = mesh.shape["space"] == TGY
    return jax.shard_map(
        per_device_paired if one_row else per_device_general,
        mesh=mesh,
        in_specs=in_specs,
        out_specs=out_specs,
        check_vma=False,
    )
```
